512 devices in a mesh: replica: 64 (over y, z), tensor: 8 (over x, core).
Axes of the slice: x: 4, y: 8, z: 8, core: 2. Of those that a mesh axis runs over, the one named last changes fastest.
Arguments:
- query_proj: bfloat16 [65536, 8192], P('replica', 'tensor'), may hold values from -100 to 100
- key_proj: bfloat16 [65536, 1024], P('replica', 'tensor'), may hold values from -100 to 100
- value_proj: bfloat16 [65536, 1024], P('replica', 'tensor'), may hold values from -6 to 6
- traj_pages: int32 [64, 4], P('replica'), may hold values from 1 to 32, 64 in all within a row
- page_dest: int32 [64, 64], P('replica'), may hold values from 0 to 63, as said below
- page_table: int32 [64, 64], P('replica'), may hold values from 0 to 63, as said below
- query_gain: float32 [128], replicated, may hold values from 0.1 to 1.9
- key_gain: float32 [128], replicated, may hold values from 0.1 to 1.9
Outputs:
- attention: bfloat16 [65536, 8192], P(('replica', 'tensor'))
- page_pool: bfloat16 [4096, 16, 2048], P('replica', None, 'tensor')
The draws below stay inside these ranges and needn't reach their ends.
Inputs may be any that keep to these rules, and one draw needn't show every extreme that they name: `page_dest`: each decoder group receives exactly 64 pages. At most 2 pages of one replica group go to one decoder group, and in every draw every replica group sends exactly 2 pages to some decoder group. `page_table`: the pages that reach one decoder group have distinct slots.
All inputs are finite; a program needn't handle non-finite values.
Results may differ from the reference program's by a relative error of at most 0.0061.
Values may be sent and summed in bfloat16 or wider, within the bound.
No kernel may reach another device: no remote copies, remote signals or barrier semaphores. Data moves between devices by JAX's collectives and lax.ppermute only.
A program may use at most 128 MiB of HBM per device.

```python
import math
import jax
import jax.numpy as jnp
import numpy as np
from jax import lax

QH = 64
KVH = 8
HD = 128
PAGE = 16
SEQS = 4
GROUP_TOK = 1024
TOKENS = 65536
PAGES = 64
MOST = 32
CAP = 2
N_REPLICA = 64


def scaled_field(key, base, top):
    left, right = jax.random.split(key)
    row_scale = jnp.exp(jax.random.uniform(left, (base.shape[0], 1), minval=0.0, maxval=math.log(top)))
    col_scale = jnp.exp(jax.random.uniform(right, (1, base.shape[1]), minval=0.0, maxval=math.log(top)))
    return (base * row_scale * col_scale / top).astype(jnp.bfloat16)


def draw_query_proj(key, part):
    key = jax.random.fold_in(key, 11)
    first_key = jax.random.fold_in(key, 0)
    third_key = jax.random.fold_in(key, 2)
    base = jnp.clip(jax.random.normal(first_key, (TOKENS, QH * HD)), -4.0, 4.0)
    return scaled_field(third_key, base, 10.0)


def draw_key_proj(key, part):
    key = jax.random.fold_in(key, 23)
    first_key = jax.random.fold_in(key, 0)
    third_key = jax.random.fold_in(key, 2)
    base = jnp.clip(jax.random.normal(first_key, (TOKENS, KVH * HD)), -4.0, 4.0)
    return scaled_field(third_key, base, 10.0)


def page_plan(key):
    key_pairs, key_order, key_offset, key_relabel, key_slots = jax.random.split(key, 5)
    groups = N_REPLICA
    page_count = PAGES
    slots_per = CAP
    fewest = max(1, -(-(page_count - groups) // (slots_per - 1)))
    largest = page_count // slots_per
    pair_count = jax.random.randint(key_pairs, (), fewest, largest + 1)
    order = jax.random.permutation(key_order, page_count)
    classes = jnp.where(order < slots_per * pair_count, order // slots_per, order - (slots_per - 1) * pair_count)
    offsets = jax.random.permutation(key_offset, groups)[classes]
    relabel = jax.random.permutation(key_relabel, groups)
    source = jnp.arange(groups, dtype=jnp.int32)[:, None]
    dest = relabel[(source + offsets[None, :]) % groups].astype(jnp.int32)
    scores = jax.random.randint(key_slots, (groups, page_count), 0, 65536) * page_count + jnp.arange(page_count, dtype=jnp.int32)[None, :]
    slot_perm = jnp.argsort(scores, axis=1).astype(jnp.int32)
    table = slot_perm[dest, jnp.arange(page_count, dtype=jnp.int32)[None, :]]
    return (dest, table.astype(jnp.int32))


def draw_page_dest(key, part):
    dest, table = page_plan(key)
    return dest


def draw_page_table(key, part):
    dest, table = page_plan(key)
    return table


def block_levels(rng, extent, pieces, least, high):
    factor_of = 1.0
    for position, parts in pieces:
        steps = jax.random.uniform(jax.random.fold_in(jax.random.fold_in(rng, 6), position), (parts,), jnp.float32, least / len(pieces), high / len(pieces))
        factor_of = factor_of * jnp.repeat(jnp.exp(steps), extent[position] // parts).reshape((-1,) + (1,) * (len(extent) - 1 - position))
    return factor_of


def split_up(count, total, bound, lean):
    loads = [(1 << 20) // math.isqrt(rank ** lean) + 1 for rank in range(2, count + 1)]
    spare, holding = total - bound - (count - 1), [1] * (count - 1)
    while spare > 0:
        free = [i for i in range(count - 1) if holding[i] < bound]
        whole, budget = sum([loads[i] for i in free]), spare
        for i in free:
            extra = min(bound - holding[i], max(1, budget * loads[i] // whole), spare)
            holding[i] = holding[i] + extra
            spare = spare - extra
    return np.array([bound] + holding)


def ragged(key, amount, total, bound, lean):
    if amount == 2:
        one = jax.random.randint(key, (), max(1, total - bound), min(bound, total - 1) + 1)
        return jnp.stack([one, total - one])
    sizes = jnp.asarray(split_up(amount, total, bound, lean), jnp.int32)
    couples = (amount - 1) // 2
    source_of, receiver = sizes[1:1 + 2 * couples:2], sizes[2:2 + 2 * couples:2]
    slack = jnp.minimum(source_of - 1, bound - receiver)
    passed = jax.random.randint(jax.random.fold_in(key, 1), (couples,), 0, 1 << 20) % (slack + 1)
    sizes = sizes.at[1:1 + 2 * couples:2].set(source_of - passed).at[2:2 + 2 * couples:2].set(receiver + passed)
    return sizes[jax.random.permutation(jax.random.fold_in(key, 2), amount)]


def gaussian(own_key, extent, spread, most, cuts=(), kind=jnp.bfloat16):
    array = jax.random.normal(own_key, extent, jnp.float32) * spread
    if len(cuts) > 0:
        array = block_levels(own_key, extent, cuts, -0.22, 0.18) * array
    return jnp.clip(array, min=-most, max=most).astype(kind)


def setup_inputs(seed: int = 0) -> dict:
    keys = jax.random.split(jax.random.key(seed), 9)
    query_proj = draw_query_proj(jax.random.fold_in(keys[8], 71), 0)
    key_proj = draw_key_proj(jax.random.fold_in(keys[8], 71), 0)
    value_proj = gaussian(keys[2], (TOKENS, KVH * HD), 1.0, 6.0, ((0, 64), (1, 8)))
    traj_pages = jax.vmap(lambda own: ragged(own, SEQS, PAGES, MOST, 0))(jax.random.split(keys[3], N_REPLICA)).reshape((N_REPLICA, SEQS)).astype(jnp.int32)
    page_dest = draw_page_dest(jax.random.fold_in(keys[8], 71), 0)
    page_table = draw_page_table(jax.random.fold_in(keys[8], 71), 0)
    query_gain = jnp.clip(1.0 + 0.18 * jax.random.normal(keys[6], (HD,), jnp.float32), 0.1, 1.9)
    key_gain = jnp.clip(1.0 + 0.18 * jax.random.normal(keys[7], (HD,), jnp.float32), 0.1, 1.9)
    return dict(query_proj=query_proj, key_proj=key_proj, value_proj=value_proj, traj_pages=traj_pages, page_dest=page_dest, page_table=page_table, query_gain=query_gain, key_gain=key_gain)


def positions(lengths, total_rows):
    token_index = jnp.arange(total_rows, dtype=jnp.int32)
    sizes = lengths.astype(jnp.int32) * PAGE
    seq_ends = jnp.cumsum(sizes)
    seq_starts = seq_ends - sizes
    segment = lax.optimization_barrier(jnp.sum((token_index[:, None] >= seq_ends[None, :]).astype(jnp.int32), axis=1))
    chosen = segment[:, None] == jnp.arange(lengths.shape[0], dtype=jnp.int32)[None, :]
    start_of = lax.optimization_barrier(jnp.sum(jnp.where(chosen, seq_starts[None, :], 0), axis=1))
    return (segment, token_index - start_of)

def norm_rope(raw, gain_vec, places):
    row_count = raw.shape[0]
    head_count = raw.shape[1] // HD
    entries = raw.astype(jnp.float32).reshape(row_count, head_count, HD)
    mean_square = lax.optimization_barrier(jnp.mean(entries * entries, axis=-1, keepdims=True))
    entries = entries * lax.rsqrt(mean_square + 1e-06) * gain_vec.astype(jnp.float32)
    half_size = HD // 2
    frequency = 1000000.0 ** (-(jnp.arange(half_size, dtype=jnp.float32) * 2.0 / HD))
    angles = places.astype(jnp.float32)[:, None] * frequency[None, :]
    cosine = jnp.cos(angles)[:, None, :]
    sine_part = jnp.sin(angles)[:, None, :]
    first_half = entries[..., :half_size]
    second = entries[..., half_size:]
    rotated = jnp.concatenate([first_half * cosine - second * sine_part, second * cosine + first_half * sine_part], axis=-1)
    return lax.optimization_barrier(rotated.astype(jnp.bfloat16)).reshape(row_count, head_count * HD)

def attend(query_rows, query_seg, query_idx, key_rows, value_rows, key_seg, key_idx):
    row_count = query_rows.shape[0]
    key_count = key_rows.shape[0]
    kv_heads = key_rows.shape[1] // HD
    group_size = query_rows.shape[1] // HD // kv_heads
    query_heads = query_rows.reshape(row_count, kv_heads, group_size, HD).astype(jnp.float32)
    key_heads = key_rows.reshape(key_count, kv_heads, HD).astype(jnp.float32)
    value_heads = value_rows.reshape(key_count, kv_heads, HD).astype(jnp.float32)
    scores = jnp.einsum('rkgd,skd->kgrs', query_heads, key_heads) * HD ** (-0.5)
    allowed = (key_seg[None, :] == query_seg[:, None]) & (key_idx[None, :] <= query_idx[:, None])
    weights = jnp.where(allowed, jnp.exp(scores), 0.0)
    denominator = lax.optimization_barrier(jnp.sum(weights, axis=-1))
    rounded = lax.optimization_barrier(weights.astype(jnp.bfloat16)).astype(jnp.float32)
    numerator = jnp.einsum('kgrs,skd->rkgd', rounded, value_heads)
    normalized = numerator / jnp.transpose(denominator, (2, 0, 1))[..., None]
    return normalized.astype(jnp.bfloat16).reshape(row_count, kv_heads * group_size * HD)

def reference(query_proj, key_proj, value_proj, traj_pages, page_dest, page_table, query_gain, key_gain):
    query_groups = query_proj.reshape(N_REPLICA, GROUP_TOK, QH * HD)
    key_groups = key_proj.reshape(N_REPLICA, GROUP_TOK, KVH * HD)
    value_groups = value_proj.reshape(N_REPLICA, GROUP_TOK, KVH * HD)

    def one_group(items):
        queries, keys_in, values_in, lengths = items
        segment, places = positions(lengths, GROUP_TOK)
        token_index = jnp.arange(GROUP_TOK, dtype=jnp.int32)
        query_ready = norm_rope(queries, query_gain, places)
        key_ready = norm_rope(keys_in, key_gain, places)
        output = attend(query_ready, segment, token_index, key_ready, values_in, segment, token_index)
        content = jnp.stack([key_ready.reshape(GROUP_TOK, KVH, HD), values_in.reshape(GROUP_TOK, KVH, HD)], axis=2)
        return (output, content.reshape(PAGES, PAGE, KVH * 2 * HD))
    output, content = lax.map(one_group, (query_groups, key_groups, value_groups, traj_pages))
    target = (page_dest.astype(jnp.int32) * PAGES + page_table.astype(jnp.int32)).reshape(-1)
    pool = jnp.zeros((N_REPLICA * PAGES, PAGE, KVH * 2 * HD), jnp.bfloat16)
    pool = pool.at[target].set(content.reshape(N_REPLICA * PAGES, PAGE, KVH * 2 * HD))
    return (output.reshape(TOKENS, QH * HD), pool)
```

```python
import functools

import jax
import jax.numpy as jnp
import numpy as np
from jax import lax
from jax.experimental import pallas as pl
from jax.experimental.pallas import tpu as pltpu
from jax.sharding import PartitionSpec as P

PAGE = 16
HD = 128
HALF = HD // 2
ROWS = 1024
BLOCK = 128
WINDOW = 256
PAGES = ROWS // PAGE
MOST = 32
HEADS = 8
HALF_ROWS = HEADS // 2 * BLOCK
GROUPS = 64
SLOTS = 2 * GROUPS
CHIPS = 4
BATCH = 8
EPS = 1e-06
LABEL_ROWS = 8
LETTER = 4 * PAGE + LABEL_ROWS
NEG = -1e30
SCALE = HD**-0.5 * np.log2(np.e)
STEPS = ((1, 0), (3, 0), (2, 0), (1, 1), (3, 1), (2, 1), (0, 1))


def rope_tables():
    frequency = 1000000.0 ** (-(np.arange(HALF) * 2.0 / HD))
    places = np.concatenate([np.arange(MOST) * PAGE, np.arange(PAGE)])
    angles = places[:, None] * frequency[None, :]
    cosine = np.concatenate([np.cos(angles)] * 2, axis=1)
    sine = np.concatenate([-np.sin(angles), np.sin(angles)], axis=1)
    return cosine.astype(np.float32), sine.astype(np.float32)


def seq_ends(traj_ref):
    first = traj_ref[0]
    second = first + traj_ref[1]
    return first, second, second + traj_ref[2]


def start_of(ends, place):
    low = jnp.int32(0)
    for end in ends:
        low = jnp.where(place >= end, end, low)
    return low


def page_rope(cos_ref, sin_ref, index):
    cos_row = cos_ref[pl.ds(index, 1), :]
    sin_row = sin_ref[pl.ds(index, 1), :]
    cos_in = cos_ref[MOST : MOST + PAGE, :]
    sin_in = sin_ref[MOST : MOST + PAGE, :]
    return cos_row * cos_in - sin_row * sin_in, sin_row * cos_in + cos_row * sin_in


def prep_kernel(
    traj_ref, dest_ref, table_ref, key_ref, value_ref, gain_ref, cos_ref, sin_ref,
    ready_ref, outbox_ref, slot_ref,
):
    ends = seq_ends(traj_ref)
    for index in range(SLOTS):
        slot_ref[index] = -1
    gain = gain_ref[...]
    gain_turned = pltpu.roll(gain, HALF, 1)
    for page in range(PAGES):
        rows = pl.ds(page * PAGE, PAGE)
        cosine, sine = page_rope(cos_ref, sin_ref, page - start_of(ends, page))
        entries = key_ref[rows, :].astype(jnp.float32)
        mean_square = jnp.mean(entries * entries, axis=-1, keepdims=True)
        turned = pltpu.roll(entries, HALF, 1)
        mixed = entries * (cosine * gain) + turned * (sine * gain_turned)
        ready = (mixed * lax.rsqrt(mean_square + EPS)).astype(jnp.bfloat16)
        ready_ref[rows, :] = ready
        dest = dest_ref[page]
        rank = jnp.where(slot_ref[dest * 2] >= 0, 1, 0)
        slot_ref[dest * 2 + rank] = table_ref[page]
        outbox_ref[dest, pl.ds(pl.multiple_of(rank * 2 * PAGE, PAGE), PAGE), :] = ready
        outbox_ref[dest, pl.ds(pl.multiple_of(rank * 2 * PAGE + PAGE, PAGE), PAGE), :] = value_ref[
            rows, :
        ]
    odd = lax.broadcasted_iota(jnp.int32, (LABEL_ROWS, HD), 1) % 2
    for dest in range(GROUPS):
        slots = jnp.where(odd == 0, slot_ref[dest * 2], slot_ref[dest * 2 + 1])
        outbox_ref[dest, LETTER - LABEL_ROWS :, :] = slots.astype(jnp.float32).astype(jnp.bfloat16)


def attend_kernel(
    block_ref, traj_ref, query_ref, key_ref, value_ref, gain_ref, cos_ref, sin_ref, *refs
):
    for index, out_ref in enumerate(refs[:-4]):
        attend_block(
            block_ref[index], traj_ref, query_ref, key_ref, value_ref, gain_ref, cos_ref, sin_ref,
            out_ref, *refs[-4:],
        )


def attend_block(
    block, traj_ref, query_ref, key_ref, value_ref, gain_ref, cos_ref, sin_ref, out_ref,
    cos_rows, sin_rows, ready, total,
):
    ends = seq_ends(traj_ref)
    gain = gain_ref[...] * SCALE
    gain_turned = pltpu.roll(gain, HALF, 1)
    for page in range(BLOCK // PAGE):
        place = block * (BLOCK // PAGE) + page
        cosine, sine = page_rope(cos_ref, sin_ref, place - start_of(ends, place))
        cos_rows[page * PAGE : (page + 1) * PAGE, :] = cosine * gain
        sin_rows[page * PAGE : (page + 1) * PAGE, :] = sine * gain_turned
    ones = jnp.ones((WINDOW, HD), jnp.bfloat16)
    lane = lax.broadcasted_iota(jnp.int32, (HD, HD), 1)
    turn = lax.broadcasted_iota(jnp.int32, (HD, HD), 0) == (lane + HALF) % HD
    turn = jnp.where(turn, 1.0, 0.0).astype(jnp.bfloat16)
    rows = pl.ds(pl.multiple_of(block * BLOCK, BLOCK), BLOCK)
    for head in range(HEADS):
        raw = query_ref[rows, head * HD : (head + 1) * HD]
        entries = raw.astype(jnp.float32)
        square = entries * entries
        upper = square.astype(jnp.bfloat16)
        lower = (square - upper.astype(jnp.float32)).astype(jnp.bfloat16)
        total_square = jnp.dot(
            jnp.concatenate([upper, lower], axis=1), ones, preferred_element_type=jnp.float32
        )
        turned = jnp.dot(raw, turn, preferred_element_type=jnp.float32)
        mixed = entries * cos_rows[...] + turned * sin_rows[...]
        scaled = mixed * lax.rsqrt(total_square * (1.0 / HD) + EPS)
        ready[head * BLOCK : (head + 1) * BLOCK, :] = scaled.astype(jnp.bfloat16)

    low = block * BLOCK
    high = low + BLOCK
    first = start_of(ends, block * (BLOCK // PAGE)) * PAGE
    windows = (high - first + WINDOW - 1) // WINDOW
    base = jnp.maximum(high - windows * WINDOW, 0)
    token = low + lax.broadcasted_iota(jnp.int32, (BLOCK, WINDOW), 0)
    begin = jnp.zeros((BLOCK, WINDOW), jnp.int32)
    for end in ends:
        begin = jnp.where(token >= end * PAGE, end * PAGE, begin)
    column = lax.broadcasted_iota(jnp.int32, (BLOCK, WINDOW), 1)

    def window(index, add):
        offset = pl.multiple_of(base + index * WINDOW, BLOCK)
        keys = key_ref[pl.ds(offset, WINDOW), :]
        values = jnp.concatenate([value_ref[pl.ds(offset, WINDOW), :], ones], axis=1)
        other = offset + column
        bias = jnp.where((other >= begin) & (other <= token), 0.0, NEG)
        for part in range(2):
            part_rows = slice(part * HALF_ROWS, (part + 1) * HALF_ROWS)
            scores = lax.dot_general(
                ready[part_rows, :], keys, (((1,), (1,)), ((), ())), preferred_element_type=jnp.float32
            )
            biased = scores.reshape(HEADS // 2, BLOCK, WINDOW) + bias[None]
            weights = jnp.exp2(biased).astype(jnp.bfloat16).reshape(HALF_ROWS, WINDOW)
            summed = jnp.dot(weights, values, preferred_element_type=jnp.float32)
            if add:
                total[part_rows, :] += summed
            else:
                total[part_rows, :] = summed

    window(0, False)
    lax.fori_loop(1, windows, lambda index, carry: (window(index, True), carry)[1], 0)
    for head in range(HEADS):
        head_rows = slice(head * BLOCK, (head + 1) * BLOCK)
        out_ref[:, head * HD : (head + 1) * HD] = (
            total[head_rows, :HD] / total[head_rows, HD:]
        ).astype(jnp.bfloat16)


def assemble_kernel(source_ref, *refs):
    count = (len(refs) - 3) // 2
    pieces, out_ref = refs[:count], refs[count]
    held, in_sems, out_sems = refs[count + 1 : count + 1 + count], refs[-2], refs[-1]
    loads, stores = [], []
    for index, piece in enumerate(pieces):
        width = piece.shape[1]
        columns = pl.ds(pl.multiple_of(source_ref[index] * width, width), width)
        loads.append(pltpu.make_async_copy(piece, held[index], in_sems.at[index]))
        stores.append(
            pltpu.make_async_copy(held[index], out_ref.at[:, columns], out_sems.at[index])
        )
    for load in loads:
        load.start()
    for load, store in zip(loads, stores):
        load.wait()
        store.start()
    for store in stores:
        store.wait()


def pool_kernel(arrived_ref, pool_ref, label_ref, slot_ref, place_ref, sem):
    lane = lax.broadcasted_iota(jnp.int32, (LABEL_ROWS, HD), 1) // 2
    labels = jnp.zeros((LABEL_ROWS, HD), jnp.float32)
    for group in range(GROUPS):
        mine = arrived_ref[group, LETTER - LABEL_ROWS :, :].astype(jnp.float32)
        labels = jnp.where(lane == group, mine, labels)
    label_ref[...] = labels.astype(jnp.int32)
    fetch = pltpu.make_async_copy(label_ref, slot_ref, sem)
    fetch.start()
    fetch.wait()
    for index in range(SLOTS):
        slot = slot_ref[0, index]
        place_ref[jnp.where(slot < 0, PAGES, slot)] = index
    for slot in range(PAGES):
        index = place_ref[slot]
        group, row = index // 2, index % 2 * (2 * PAGE)
        for half in range(2):
            rows = pl.ds(pl.multiple_of(row + half * PAGE, PAGE), PAGE)
            pool_ref[slot, :, half * HD : (half + 1) * HD] = arrived_ref[group, rows, :]


VMEM = pl.BlockSpec(memory_space=pltpu.VMEM)
SMEM = pl.BlockSpec(memory_space=pltpu.SMEM)
ANY = pl.BlockSpec(memory_space=pl.ANY)
ATTEND_VMEM = 12 << 20
PARAMS = pltpu.CompilerParams(vmem_limit_bytes=63 << 20)


def cost(flops, moved):
    return pl.CostEstimate(flops=flops, bytes_accessed=moved, transcendentals=0)


def prep(traj, dest, table, key_proj, value_proj, gain, cosine, sine):
    return pl.pallas_call(
        prep_kernel,
        out_shape=(
            jax.ShapeDtypeStruct((ROWS, HD), jnp.bfloat16),
            jax.ShapeDtypeStruct((GROUPS, LETTER, HD), jnp.bfloat16),
        ),
        in_specs=[SMEM] * 3 + [VMEM] * 5,
        out_specs=(VMEM, VMEM),
        scratch_shapes=[pltpu.SMEM((SLOTS,), jnp.int32)],
        compiler_params=PARAMS,
        cost_estimate=cost(10**6, 4 << 20),
        name="prep",
    )(traj, dest, table, key_proj, value_proj, gain, cosine, sine)


def attend(blocks, traj, query_proj, ready, value_proj, gain, cosine, sine):
    return pl.pallas_call(
        attend_kernel,
        out_shape=[jax.ShapeDtypeStruct((BLOCK, HEADS * HD), jnp.bfloat16)] * len(blocks),
        in_specs=[SMEM] * 2 + [VMEM] * 6,
        out_specs=[VMEM] * len(blocks),
        scratch_shapes=[
            pltpu.VMEM((BLOCK, HD), jnp.float32),
            pltpu.VMEM((BLOCK, HD), jnp.float32),
            pltpu.VMEM((HEADS * BLOCK, HD), jnp.bfloat16),
            pltpu.VMEM((HEADS * BLOCK, 2 * HD), jnp.float32),
        ],
        compiler_params=pltpu.CompilerParams(vmem_limit_bytes=ATTEND_VMEM),
        cost_estimate=cost(len(blocks) * 400 * 10**6, 4 << 20),
        name="attend",
    )(jnp.stack(blocks), traj, query_proj, ready, value_proj, gain, cosine, sine)


def assemble(sources, pieces):
    rows, width = pieces[0].shape
    return pl.pallas_call(
        assemble_kernel,
        out_shape=jax.ShapeDtypeStruct((rows, width * len(pieces)), jnp.bfloat16),
        in_specs=[SMEM] + [ANY] * len(pieces),
        out_specs=ANY,
        scratch_shapes=[pltpu.VMEM(piece.shape, piece.dtype) for piece in pieces]
        + [pltpu.SemaphoreType.DMA((len(pieces),))] * 2,
        compiler_params=PARAMS,
        cost_estimate=cost(10**6, 4 << 20),
        name="assemble",
    )(sources, *pieces)


def fill_pool(arrived):
    return pl.pallas_call(
        pool_kernel,
        out_shape=jax.ShapeDtypeStruct((PAGES, PAGE, 2 * HD), jnp.bfloat16),
        in_specs=[VMEM],
        out_specs=VMEM,
        scratch_shapes=[
            pltpu.VMEM((LABEL_ROWS, HD), jnp.int32),
            pltpu.SMEM((LABEL_ROWS, HD), jnp.int32),
            pltpu.SMEM((PAGES + 1,), jnp.int32),
            pltpu.SemaphoreType.DMA,
        ],
        compiler_params=PARAMS,
        cost_estimate=cost(10**6, 2 << 20),
        name="pool",
    )(arrived)


def shards(
    query_proj, key_proj, value_proj, traj_pages, page_dest, page_table, query_gain, key_gain
):
    cosine, sine = (jnp.asarray(table) for table in rope_tables())
    traj, dest, table = traj_pages[0], page_dest[0], page_table[0]
    query_gain, key_gain = query_gain[None, :], key_gain[None, :]
    ready, outbox = prep(traj, dest, table, key_proj, value_proj, key_gain, cosine, sine)
    arrived = lax.all_to_all(outbox, "replica", split_axis=0, concat_axis=0, tiled=True)

    me = lax.axis_index("tensor")
    chip, core = me // 2, me % 2
    targets = [(chip + step) % CHIPS * 2 + (core ^ flip) for step, flip in STEPS] + [me]
    sources = [(chip - step + CHIPS) % CHIPS * 2 + (core ^ flip) for step, flip in STEPS] + [me]
    pieces = []
    for begin in range(0, len(targets), BATCH):
        pieces += attend(
            targets[begin : begin + BATCH], traj, query_proj, ready, value_proj, query_gain, cosine, sine
        )
    for index, (step, flip) in enumerate(STEPS):
        pairs = [
            (x * 2 + c, (x + step) % CHIPS * 2 + (c ^ flip)) for x in range(CHIPS) for c in range(2)
        ]
        pieces[index] = lax.ppermute(pieces[index], "tensor", pairs)
    return assemble(jnp.stack(sources), pieces), fill_pool(arrived)


def solution(mesh):
    in_specs = (
        P("replica", "tensor"),
        P("replica", "tensor"),
        P("replica", "tensor"),
        P("replica", None),
        P("replica", None),
        P("replica", None),
        P(),
        P(),
    )
    out_specs = (P(("replica", "tensor"), None), P("replica", None, "tensor"))
    return jax.shard_map(shards, mesh=mesh, in_specs=in_specs, out_specs=out_specs, check_vma=False)
```

```python
import functools

import jax
import jax.numpy as jnp
import numpy as np
from jax import lax
from jax.experimental import pallas as pl
from jax.experimental.pallas import tpu as pltpu
from jax.sharding import PartitionSpec as P

PAGE = 16
HD = 128
HALF = HD // 2
ROWS = 1024
BLOCK = 128
WINDOW = 256
PAGES = ROWS // PAGE
MOST = 32
HEADS = 8
HALF_ROWS = HEADS // 2 * BLOCK
GROUPS = 64
SLOTS = 2 * GROUPS
CHIPS = 4
BATCHES = (8,)
EPS = 1e-06
LABEL_ROWS = 8
LETTER = 4 * PAGE + LABEL_ROWS
NEG = -1e30
SCALE = HD**-0.5 * np.log2(np.e)
STEPS = ((1, 0), (3, 0), (2, 0), (1, 1), (3, 1), (2, 1), (0, 1), (0, 0))


def rope_tables():
    frequency = 1000000.0 ** (-(np.arange(HALF) * 2.0 / HD))
    places = np.concatenate([np.arange(MOST) * PAGE, np.arange(PAGE)])
    angles = places[:, None] * frequency[None, :]
    cosine = np.concatenate([np.cos(angles)] * 2, axis=1)
    sine = np.concatenate([-np.sin(angles), np.sin(angles)], axis=1)
    return cosine.astype(np.float32), sine.astype(np.float32)


def target_of(me, step, flip):
    return ((((me >> 1) + step) & (CHIPS - 1)) << 1) | ((me & 1) ^ flip)


def source_of(me, step, flip):
    return target_of(me, CHIPS - step, flip)


def seq_ends(traj_ref):
    first = traj_ref[0]
    second = first + traj_ref[1]
    return first, second, second + traj_ref[2]


def start_of(ends, place):
    low = jnp.int32(0)
    for end in ends:
        low = jnp.where(place >= end, end, low)
    return low


def page_rope(cos_ref, sin_ref, index):
    cos_row = cos_ref[pl.ds(index, 1), :]
    sin_row = sin_ref[pl.ds(index, 1), :]
    cos_in = cos_ref[MOST : MOST + PAGE, :]
    sin_in = sin_ref[MOST : MOST + PAGE, :]
    return cos_row * cos_in - sin_row * sin_in, sin_row * cos_in + cos_row * sin_in


def prep_kernel(
    traj_ref, dest_ref, table_ref, key_ref, value_ref, gain_ref, cos_ref, sin_ref,
    ready_ref, outbox_ref, slot_ref,
):
    ends = seq_ends(traj_ref)
    for index in range(SLOTS):
        slot_ref[index] = -1
    gain = gain_ref[...]
    gain_turned = pltpu.roll(gain, HALF, 1)
    for page in range(PAGES):
        rows = pl.ds(page * PAGE, PAGE)
        cosine, sine = page_rope(cos_ref, sin_ref, page - start_of(ends, page))
        entries = key_ref[rows, :].astype(jnp.float32)
        mean_square = jnp.mean(entries * entries, axis=-1, keepdims=True)
        turned = pltpu.roll(entries, HALF, 1)
        mixed = entries * (cosine * gain) + turned * (sine * gain_turned)
        ready = (mixed * lax.rsqrt(mean_square + EPS)).astype(jnp.bfloat16)
        ready_ref[rows, :] = ready
        dest = dest_ref[page]
        rank = jnp.where(slot_ref[dest * 2] >= 0, 1, 0)
        slot_ref[dest * 2 + rank] = table_ref[page]
        outbox_ref[dest, pl.ds(pl.multiple_of(rank * 2 * PAGE, PAGE), PAGE), :] = ready
        outbox_ref[dest, pl.ds(pl.multiple_of(rank * 2 * PAGE + PAGE, PAGE), PAGE), :] = value_ref[
            rows, :
        ]
    odd = lax.broadcasted_iota(jnp.int32, (LABEL_ROWS, HD), 1) % 2
    for dest in range(GROUPS):
        slots = jnp.where(odd == 0, slot_ref[dest * 2], slot_ref[dest * 2 + 1])
        outbox_ref[dest, LETTER - LABEL_ROWS :, :] = slots.astype(jnp.float32).astype(jnp.bfloat16)


def attend_kernel(
    steps, me_ref, traj_ref, query_ref, key_ref, value_ref, gain_ref, cos_ref, sin_ref, *refs
):
    out_refs, next_ref, scratch = refs[: len(steps)], refs[len(steps)], refs[len(steps) + 1 :]
    next_ref[0] = me_ref[0]
    for (step, flip), out_ref in zip(steps, out_refs):
        attend_block(
            target_of(me_ref[0], step, flip), traj_ref, query_ref, key_ref, value_ref, gain_ref,
            cos_ref, sin_ref, out_ref, *scratch,
        )


def attend_block(
    block, traj_ref, query_ref, key_ref, value_ref, gain_ref, cos_ref, sin_ref, out_ref,
    cos_rows, sin_rows, ready, total,
):
    ends = seq_ends(traj_ref)
    gain = gain_ref[...] * SCALE
    gain_turned = pltpu.roll(gain, HALF, 1)
    for page in range(BLOCK // PAGE):
        place = block * (BLOCK // PAGE) + page
        cosine, sine = page_rope(cos_ref, sin_ref, place - start_of(ends, place))
        cos_rows[page * PAGE : (page + 1) * PAGE, :] = cosine * gain
        sin_rows[page * PAGE : (page + 1) * PAGE, :] = sine * gain_turned
    ones = jnp.ones((WINDOW, HD), jnp.bfloat16)
    lane = lax.broadcasted_iota(jnp.int32, (HD, HD), 1)
    turn = lax.broadcasted_iota(jnp.int32, (HD, HD), 0) == (lane + HALF) % HD
    turn = jnp.where(turn, 1.0, 0.0).astype(jnp.bfloat16)
    rows = pl.ds(pl.multiple_of(block * BLOCK, BLOCK), BLOCK)
    for head in range(HEADS):
        raw = query_ref[rows, head * HD : (head + 1) * HD]
        entries = raw.astype(jnp.float32)
        square = (entries * entries).astype(jnp.bfloat16)
        total_square = jnp.dot(square, ones[:HD], preferred_element_type=jnp.float32)
        turned = jnp.dot(raw, turn, preferred_element_type=jnp.float32)
        mixed = entries * cos_rows[...] + turned * sin_rows[...]
        scaled = mixed * lax.rsqrt(total_square * (1.0 / HD) + EPS)
        ready[head * BLOCK : (head + 1) * BLOCK, :] = scaled.astype(jnp.bfloat16)

    low = block * BLOCK
    high = low + BLOCK
    first = start_of(ends, block * (BLOCK // PAGE)) * PAGE
    windows = (high - first + WINDOW - 1) // WINDOW
    base = jnp.maximum(high - windows * WINDOW, 0)
    token = low + lax.broadcasted_iota(jnp.int32, (BLOCK, WINDOW), 0)
    begin = jnp.zeros((BLOCK, WINDOW), jnp.int32)
    for end in ends:
        begin = jnp.where(token >= end * PAGE, end * PAGE, begin)
    column = lax.broadcasted_iota(jnp.int32, (BLOCK, WINDOW), 1)

    def window(index, add):
        offset = pl.multiple_of(base + index * WINDOW, BLOCK)
        keys = key_ref[pl.ds(offset, WINDOW), :]
        values = jnp.concatenate([value_ref[pl.ds(offset, WINDOW), :], ones], axis=1)
        other = offset + column
        bias = jnp.where((other >= begin) & (other <= token), 0.0, NEG)
        for part in range(2):
            part_rows = slice(part * HALF_ROWS, (part + 1) * HALF_ROWS)
            scores = lax.dot_general(
                ready[part_rows, :], keys, (((1,), (1,)), ((), ())), preferred_element_type=jnp.float32
            )
            biased = scores.reshape(HEADS // 2, BLOCK, WINDOW) + bias[None]
            weights = jnp.exp2(biased).astype(jnp.bfloat16).reshape(HALF_ROWS, WINDOW)
            summed = jnp.dot(weights, values, preferred_element_type=jnp.float32)
            if add:
                total[part_rows, :] += summed
            else:
                total[part_rows, :] = summed

    window(0, False)
    lax.fori_loop(1, windows, lambda index, carry: (window(index, True), carry)[1], 0)
    for head in range(HEADS):
        head_rows = slice(head * BLOCK, (head + 1) * BLOCK)
        out_ref[:, head * HD : (head + 1) * HD] = (
            total[head_rows, :HD] / total[head_rows, HD:]
        ).astype(jnp.bfloat16)


def assemble_kernel(me_ref, *refs):
    pieces, out_ref, sems = refs[:-2], refs[-2], refs[-1]
    copies = []
    for index, (piece, (step, flip)) in enumerate(zip(pieces, STEPS)):
        width = piece.shape[1]
        start = pl.multiple_of(source_of(me_ref[0], step, flip) * width, width)
        copies.append(
            pltpu.make_async_copy(piece, out_ref.at[:, pl.ds(start, width)], sems.at[index])
        )
    for copy in copies:
        copy.start()
    for copy in copies:
        copy.wait()


def pool_kernel(source_ref, pool_ref, arrived_ref, label_ref, slot_ref, place_ref, sem):
    load = pltpu.make_async_copy(source_ref, arrived_ref, sem)
    load.start()
    load.wait()
    lane = lax.broadcasted_iota(jnp.int32, (LABEL_ROWS, HD), 1) // 2
    labels = jnp.zeros((LABEL_ROWS, HD), jnp.float32)
    for group in range(GROUPS):
        mine = arrived_ref[group, LETTER - LABEL_ROWS :, :].astype(jnp.float32)
        labels = jnp.where(lane == group, mine, labels)
    label_ref[...] = labels.astype(jnp.int32)
    fetch = pltpu.make_async_copy(label_ref, slot_ref, sem)
    fetch.start()
    fetch.wait()
    for index in range(SLOTS):
        slot = slot_ref[0, index]
        place_ref[jnp.where(slot < 0, PAGES, slot)] = index
    for slot in range(PAGES):
        index = place_ref[slot]
        group, row = index // 2, index % 2 * (2 * PAGE)
        for half in range(2):
            rows = pl.ds(pl.multiple_of(row + half * PAGE, PAGE), PAGE)
            pool_ref[slot, :, half * HD : (half + 1) * HD] = arrived_ref[group, rows, :]


VMEM = pl.BlockSpec(memory_space=pltpu.VMEM)
SMEM = pl.BlockSpec(memory_space=pltpu.SMEM)
ANY = pl.BlockSpec(memory_space=pl.ANY)
HBM = pl.BlockSpec(memory_space=pltpu.HBM)
ATTEND_VMEM = 12 << 20
TAIL_VMEM = 8 << 20
PARAMS = pltpu.CompilerParams(vmem_limit_bytes=63 << 20)


def cost(flops, moved):
    return pl.CostEstimate(flops=flops, bytes_accessed=moved, transcendentals=0)


def prep(traj, dest, table, key_proj, value_proj, gain, cosine, sine):
    return pl.pallas_call(
        prep_kernel,
        out_shape=(
            jax.ShapeDtypeStruct((ROWS, HD), jnp.bfloat16),
            jax.ShapeDtypeStruct((GROUPS, LETTER, HD), jnp.bfloat16),
        ),
        in_specs=[SMEM] * 3 + [VMEM] * 5,
        out_specs=(VMEM, VMEM),
        scratch_shapes=[pltpu.SMEM((SLOTS,), jnp.int32)],
        compiler_params=PARAMS,
        cost_estimate=cost(10**6, 4 << 20),
        name="prep",
    )(traj, dest, table, key_proj, value_proj, gain, cosine, sine)


def attend(steps, me, traj, query_proj, ready, value_proj, gain, cosine, sine):
    return pl.pallas_call(
        functools.partial(attend_kernel, steps),
        out_shape=[jax.ShapeDtypeStruct((BLOCK, HEADS * HD), jnp.bfloat16)] * len(steps)
        + [jax.ShapeDtypeStruct((1,), jnp.int32)],
        in_specs=[SMEM] * 2 + [VMEM] * 6,
        out_specs=[VMEM] * len(steps) + [SMEM],
        scratch_shapes=[
            pltpu.VMEM((BLOCK, HD), jnp.float32),
            pltpu.VMEM((BLOCK, HD), jnp.float32),
            pltpu.VMEM((HEADS * BLOCK, HD), jnp.bfloat16),
            pltpu.VMEM((HEADS * BLOCK, 2 * HD), jnp.float32),
        ],
        compiler_params=pltpu.CompilerParams(vmem_limit_bytes=ATTEND_VMEM),
        cost_estimate=cost(len(steps) * 400 * 10**6, 4 << 20),
        name="attend",
    )(me, traj, query_proj, ready, value_proj, gain, cosine, sine)


def assemble(me, pieces):
    rows, width = pieces[0].shape
    return pl.pallas_call(
        assemble_kernel,
        out_shape=jax.ShapeDtypeStruct((rows, width * len(pieces)), jnp.bfloat16),
        in_specs=[SMEM] + [VMEM] * len(pieces),
        out_specs=ANY,
        scratch_shapes=[pltpu.SemaphoreType.DMA((len(pieces),))],
        compiler_params=pltpu.CompilerParams(vmem_limit_bytes=TAIL_VMEM),
        cost_estimate=cost(10**6, 4 << 20),
        name="assemble",
    )(me, *pieces)


def fill_pool(arrived):
    return pl.pallas_call(
        pool_kernel,
        out_shape=jax.ShapeDtypeStruct((PAGES, PAGE, 2 * HD), jnp.bfloat16),
        in_specs=[HBM],
        out_specs=VMEM,
        scratch_shapes=[
            pltpu.VMEM(arrived.shape, arrived.dtype),
            pltpu.VMEM((LABEL_ROWS, HD), jnp.int32),
            pltpu.SMEM((LABEL_ROWS, HD), jnp.int32),
            pltpu.SMEM((PAGES + 1,), jnp.int32),
            pltpu.SemaphoreType.DMA,
        ],
        compiler_params=pltpu.CompilerParams(vmem_limit_bytes=TAIL_VMEM),
        cost_estimate=cost(10**6, 2 << 20),
        name="pool",
    )(arrived)


def shards(
    query_proj, key_proj, value_proj, traj_pages, page_dest, page_table, query_gain, key_gain
):
    cosine, sine = (jnp.asarray(table) for table in rope_tables())
    traj, dest, table = traj_pages[0], page_dest[0], page_table[0]
    query_gain, key_gain = query_gain[None, :], key_gain[None, :]
    ready, outbox = prep(traj, dest, table, key_proj, value_proj, key_gain, cosine, sine)
    arrived = lax.all_to_all(outbox, "replica", split_axis=0, concat_axis=0, tiled=True)

    me = lax.axis_index("tensor").astype(jnp.int32).reshape(1)
    pieces, first = [], 0
    for count in BATCHES:
        steps = STEPS[first : first + count]
        *parts, me = attend(steps, me, traj, query_proj, ready, value_proj, query_gain, cosine, sine)
        for (step, flip), piece in zip(steps, parts):
            pairs = [
                (x * 2 + c, (x + step) % CHIPS * 2 + (c ^ flip))
                for x in range(CHIPS)
                for c in range(2)
            ]
            pieces.append(lax.ppermute(piece, "tensor", pairs) if step or flip else piece)
        first += count
    pool, me = lax.optimization_barrier((fill_pool(arrived), me))
    return assemble(me, pieces), pool


def solution(mesh):
    in_specs = (
        P("replica", "tensor"),
        P("replica", "tensor"),
        P("replica", "tensor"),
        P("replica", None),
        P("replica", None),
        P("replica", None),
        P(),
        P(),
    )
    out_specs = (P(("replica", "tensor"), None), P("replica", None, "tensor"))
    return jax.shard_map(shards, mesh=mesh, in_specs=in_specs, out_specs=out_specs, check_vma=False)
```

```python
import functools

import jax
import jax.numpy as jnp
import numpy as np
from jax import lax
from jax.experimental import pallas as pl
from jax.experimental.pallas import tpu as pltpu
from jax.sharding import PartitionSpec as P

PAGE = 16
HD = 128
HALF = HD // 2
ROWS = 1024
BLOCK = 128
WINDOW = 256
PAGES = ROWS // PAGE
MOST = 32
HEADS = 8
HALF_ROWS = HEADS // 2 * BLOCK
GROUPS = 64
SLOTS = 2 * GROUPS
CHIPS = 4
BATCHES = (8,)
EPS = 1e-06
LABEL_ROWS = 8
LETTER = 4 * PAGE + LABEL_ROWS
NEG = -1e30
SCALE = HD**-0.5 * np.log2(np.e)
STEPS = ((2, 0), (2, 1), (1, 0), (3, 0), (1, 1), (3, 1), (0, 1), (0, 0))


def rope_tables():
    frequency = 1000000.0 ** (-(np.arange(HALF) * 2.0 / HD))
    places = np.concatenate([np.arange(MOST) * PAGE, np.arange(PAGE)])
    angles = places[:, None] * frequency[None, :]
    cosine = np.concatenate([np.cos(angles)] * 2, axis=1)
    sine = np.concatenate([-np.sin(angles), np.sin(angles)], axis=1)
    return cosine.astype(np.float32), sine.astype(np.float32)


def target_of(me, step, flip):
    return ((((me >> 1) + step) & (CHIPS - 1)) << 1) | ((me & 1) ^ flip)


def source_of(me, step, flip):
    return target_of(me, CHIPS - step, flip)


def seq_ends(traj_ref):
    first = traj_ref[0]
    second = first + traj_ref[1]
    return first, second, second + traj_ref[2]


def start_of(ends, place):
    low = jnp.int32(0)
    for end in ends:
        low = jnp.where(place >= end, end, low)
    return low


def page_rope(cos_ref, sin_ref, index):
    cos_row = cos_ref[pl.ds(index, 1), :]
    sin_row = sin_ref[pl.ds(index, 1), :]
    cos_in = cos_ref[MOST : MOST + PAGE, :]
    sin_in = sin_ref[MOST : MOST + PAGE, :]
    return cos_row * cos_in - sin_row * sin_in, sin_row * cos_in + cos_row * sin_in


def prep_kernel(
    traj_ref, dest_ref, table_ref, key_ref, value_ref, gain_ref, cos_ref, sin_ref,
    ready_ref, outbox_ref, slot_ref,
):
    ends = seq_ends(traj_ref)
    for index in range(SLOTS):
        slot_ref[index] = -1
    gain = gain_ref[...]
    gain_turned = pltpu.roll(gain, HALF, 1)
    for page in range(PAGES):
        rows = pl.ds(page * PAGE, PAGE)
        cosine, sine = page_rope(cos_ref, sin_ref, page - start_of(ends, page))
        entries = key_ref[rows, :].astype(jnp.float32)
        mean_square = jnp.mean(entries * entries, axis=-1, keepdims=True)
        turned = pltpu.roll(entries, HALF, 1)
        mixed = entries * (cosine * gain) + turned * (sine * gain_turned)
        ready = (mixed * lax.rsqrt(mean_square + EPS)).astype(jnp.bfloat16)
        ready_ref[rows, :] = ready
        dest = dest_ref[page]
        rank = jnp.where(slot_ref[dest * 2] >= 0, 1, 0)
        slot_ref[dest * 2 + rank] = table_ref[page]
        outbox_ref[dest, pl.ds(pl.multiple_of(rank * 2 * PAGE, PAGE), PAGE), :] = ready
        outbox_ref[dest, pl.ds(pl.multiple_of(rank * 2 * PAGE + PAGE, PAGE), PAGE), :] = value_ref[
            rows, :
        ]
    odd = lax.broadcasted_iota(jnp.int32, (LABEL_ROWS, HD), 1) % 2
    for dest in range(GROUPS):
        slots = jnp.where(odd == 0, slot_ref[dest * 2], slot_ref[dest * 2 + 1])
        outbox_ref[dest, LETTER - LABEL_ROWS :, :] = slots.astype(jnp.float32).astype(jnp.bfloat16)


def attend_kernel(
    steps, me_ref, traj_ref, query_ref, key_ref, value_ref, gain_ref, cos_ref, sin_ref, *refs
):
    out_refs, next_ref, scratch = refs[: len(steps)], refs[len(steps)], refs[len(steps) + 1 :]
    next_ref[0] = me_ref[0]
    for (step, flip), out_ref in zip(steps, out_refs):
        attend_block(
            target_of(me_ref[0], step, flip), traj_ref, query_ref, key_ref, value_ref, gain_ref,
            cos_ref, sin_ref, out_ref, *scratch,
        )


def attend_block(
    block, traj_ref, query_ref, key_ref, value_ref, gain_ref, cos_ref, sin_ref, out_ref,
    cos_rows, sin_rows, ready, total,
):
    ends = seq_ends(traj_ref)
    gain = gain_ref[...] * SCALE
    gain_turned = pltpu.roll(gain, HALF, 1)
    for page in range(BLOCK // PAGE):
        place = block * (BLOCK // PAGE) + page
        cosine, sine = page_rope(cos_ref, sin_ref, place - start_of(ends, place))
        cos_rows[page * PAGE : (page + 1) * PAGE, :] = cosine * gain
        sin_rows[page * PAGE : (page + 1) * PAGE, :] = sine * gain_turned
    ones = jnp.ones((WINDOW, HD), jnp.bfloat16)
    lane = lax.broadcasted_iota(jnp.int32, (HD, HD), 1)
    turn = lax.broadcasted_iota(jnp.int32, (HD, HD), 0) == (lane + HALF) % HD
    turn = jnp.where(turn, 1.0, 0.0).astype(jnp.bfloat16)
    rows = pl.ds(pl.multiple_of(block * BLOCK, BLOCK), BLOCK)
    for head in range(HEADS):
        raw = query_ref[rows, head * HD : (head + 1) * HD]
        entries = raw.astype(jnp.float32)
        square = (entries * entries).astype(jnp.bfloat16)
        total_square = jnp.dot(square, ones[:HD], preferred_element_type=jnp.float32)
        turned = jnp.dot(raw, turn, preferred_element_type=jnp.float32)
        mixed = entries * cos_rows[...] + turned * sin_rows[...]
        scaled = mixed * lax.rsqrt(total_square * (1.0 / HD) + EPS)
        ready[head * BLOCK : (head + 1) * BLOCK, :] = scaled.astype(jnp.bfloat16)

    low = block * BLOCK
    high = low + BLOCK
    first = start_of(ends, block * (BLOCK // PAGE)) * PAGE
    windows = (high - first + WINDOW - 1) // WINDOW
    base = jnp.maximum(high - windows * WINDOW, 0)
    token = low + lax.broadcasted_iota(jnp.int32, (BLOCK, WINDOW), 0)
    begin = jnp.zeros((BLOCK, WINDOW), jnp.int32)
    for end in ends:
        begin = jnp.where(token >= end * PAGE, end * PAGE, begin)
    column = lax.broadcasted_iota(jnp.int32, (BLOCK, WINDOW), 1)

    def window(index, add):
        offset = pl.multiple_of(base + index * WINDOW, BLOCK)
        keys = key_ref[pl.ds(offset, WINDOW), :]
        values = jnp.concatenate([value_ref[pl.ds(offset, WINDOW), :], ones], axis=1)
        other = offset + column
        bias = jnp.where((other >= begin) & (other <= token), 0.0, NEG)
        for part in range(2):
            part_rows = slice(part * HALF_ROWS, (part + 1) * HALF_ROWS)
            scores = lax.dot_general(
                ready[part_rows, :], keys, (((1,), (1,)), ((), ())), preferred_element_type=jnp.float32
            )
            biased = scores.reshape(HEADS // 2, BLOCK, WINDOW) + bias[None]
            weights = jnp.exp2(biased).astype(jnp.bfloat16).reshape(HALF_ROWS, WINDOW)
            summed = jnp.dot(weights, values, preferred_element_type=jnp.float32)
            if add:
                total[part_rows, :] += summed
            else:
                total[part_rows, :] = summed

    window(0, False)
    lax.fori_loop(1, windows, lambda index, carry: (window(index, True), carry)[1], 0)
    for head in range(HEADS):
        head_rows = slice(head * BLOCK, (head + 1) * BLOCK)
        out_ref[:, head * HD : (head + 1) * HD] = (
            total[head_rows, :HD] / total[head_rows, HD:]
        ).astype(jnp.bfloat16)


def assemble_kernel(me_ref, *refs):
    pieces, out_ref, sems = refs[:-2], refs[-2], refs[-1]
    copies = []
    for index, (piece, (step, flip)) in enumerate(zip(pieces, STEPS)):
        width = piece.shape[1]
        start = pl.multiple_of(source_of(me_ref[0], step, flip) * width, width)
        copies.append(
            pltpu.make_async_copy(piece, out_ref.at[:, pl.ds(start, width)], sems.at[index])
        )
    for copy in copies:
        copy.start()
    for copy in copies:
        copy.wait()


def pool_kernel(source_ref, pool_ref, arrived_ref, label_ref, slot_ref, place_ref, sem):
    load = pltpu.make_async_copy(source_ref, arrived_ref, sem)
    load.start()
    load.wait()
    lane = lax.broadcasted_iota(jnp.int32, (LABEL_ROWS, HD), 1) // 2
    labels = jnp.zeros((LABEL_ROWS, HD), jnp.float32)
    for group in range(GROUPS):
        mine = arrived_ref[group, LETTER - LABEL_ROWS :, :].astype(jnp.float32)
        labels = jnp.where(lane == group, mine, labels)
    label_ref[...] = labels.astype(jnp.int32)
    fetch = pltpu.make_async_copy(label_ref, slot_ref, sem)
    fetch.start()
    fetch.wait()
    for index in range(SLOTS):
        slot = slot_ref[0, index]
        place_ref[jnp.where(slot < 0, PAGES, slot)] = index
    for slot in range(PAGES):
        index = place_ref[slot]
        group, row = index // 2, index % 2 * (2 * PAGE)
        for half in range(2):
            rows = pl.ds(pl.multiple_of(row + half * PAGE, PAGE), PAGE)
            pool_ref[slot, :, half * HD : (half + 1) * HD] = arrived_ref[group, rows, :]


VMEM = pl.BlockSpec(memory_space=pltpu.VMEM)
SMEM = pl.BlockSpec(memory_space=pltpu.SMEM)
ANY = pl.BlockSpec(memory_space=pl.ANY)
HBM = pl.BlockSpec(memory_space=pltpu.HBM)
ATTEND_VMEM = 12 << 20
TAIL_VMEM = 8 << 20
PARAMS = pltpu.CompilerParams(vmem_limit_bytes=63 << 20)


def cost(flops, moved):
    return pl.CostEstimate(flops=flops, bytes_accessed=moved, transcendentals=0)


def prep(traj, dest, table, key_proj, value_proj, gain, cosine, sine):
    return pl.pallas_call(
        prep_kernel,
        out_shape=(
            jax.ShapeDtypeStruct((ROWS, HD), jnp.bfloat16),
            jax.ShapeDtypeStruct((GROUPS, LETTER, HD), jnp.bfloat16),
        ),
        in_specs=[SMEM] * 3 + [VMEM] * 5,
        out_specs=(VMEM, VMEM),
        scratch_shapes=[pltpu.SMEM((SLOTS,), jnp.int32)],
        compiler_params=PARAMS,
        cost_estimate=cost(10**6, 4 << 20),
        name="prep",
    )(traj, dest, table, key_proj, value_proj, gain, cosine, sine)


def attend(steps, me, traj, query_proj, ready, value_proj, gain, cosine, sine):
    return pl.pallas_call(
        functools.partial(attend_kernel, steps),
        out_shape=[jax.ShapeDtypeStruct((BLOCK, HEADS * HD), jnp.bfloat16)] * len(steps)
        + [jax.ShapeDtypeStruct((1,), jnp.int32)],
        in_specs=[SMEM] * 2 + [VMEM] * 6,
        out_specs=[VMEM] * len(steps) + [SMEM],
        scratch_shapes=[
            pltpu.VMEM((BLOCK, HD), jnp.float32),
            pltpu.VMEM((BLOCK, HD), jnp.float32),
            pltpu.VMEM((HEADS * BLOCK, HD), jnp.bfloat16),
            pltpu.VMEM((HEADS * BLOCK, 2 * HD), jnp.float32),
        ],
        compiler_params=pltpu.CompilerParams(vmem_limit_bytes=ATTEND_VMEM),
        cost_estimate=cost(len(steps) * 400 * 10**6, 4 << 20),
        name="attend",
    )(me, traj, query_proj, ready, value_proj, gain, cosine, sine)


def assemble(me, pieces):
    rows, width = pieces[0].shape
    return pl.pallas_call(
        assemble_kernel,
        out_shape=jax.ShapeDtypeStruct((rows, width * len(pieces)), jnp.bfloat16),
        in_specs=[SMEM] + [VMEM] * len(pieces),
        out_specs=ANY,
        scratch_shapes=[pltpu.SemaphoreType.DMA((len(pieces),))],
        compiler_params=pltpu.CompilerParams(vmem_limit_bytes=TAIL_VMEM),
        cost_estimate=cost(10**6, 4 << 20),
        name="assemble",
    )(me, *pieces)


def fill_pool(arrived):
    return pl.pallas_call(
        pool_kernel,
        out_shape=jax.ShapeDtypeStruct((PAGES, PAGE, 2 * HD), jnp.bfloat16),
        in_specs=[HBM],
        out_specs=VMEM,
        scratch_shapes=[
            pltpu.VMEM(arrived.shape, arrived.dtype),
            pltpu.VMEM((LABEL_ROWS, HD), jnp.int32),
            pltpu.SMEM((LABEL_ROWS, HD), jnp.int32),
            pltpu.SMEM((PAGES + 1,), jnp.int32),
            pltpu.SemaphoreType.DMA,
        ],
        compiler_params=pltpu.CompilerParams(vmem_limit_bytes=TAIL_VMEM),
        cost_estimate=cost(10**6, 2 << 20),
        name="pool",
    )(arrived)


def shards(
    query_proj, key_proj, value_proj, traj_pages, page_dest, page_table, query_gain, key_gain
):
    cosine, sine = (jnp.asarray(table) for table in rope_tables())
    traj, dest, table = traj_pages[0], page_dest[0], page_table[0]
    query_gain, key_gain = query_gain[None, :], key_gain[None, :]
    ready, outbox = prep(traj, dest, table, key_proj, value_proj, key_gain, cosine, sine)
    arrived = lax.all_to_all(outbox, "replica", split_axis=0, concat_axis=0, tiled=True)
    arrived = pltpu.with_memory_space_constraint(arrived, pltpu.HBM)

    me = lax.axis_index("tensor").astype(jnp.int32).reshape(1)
    pieces, first = [], 0
    for count in BATCHES:
        steps = STEPS[first : first + count]
        *parts, me = attend(steps, me, traj, query_proj, ready, value_proj, query_gain, cosine, sine)
        for (step, flip), piece in zip(steps, parts):
            pairs = [
                (x * 2 + c, (x + step) % CHIPS * 2 + (c ^ flip))
                for x in range(CHIPS)
                for c in range(2)
            ]
            pieces.append(lax.ppermute(piece, "tensor", pairs) if step or flip else piece)
        first += count
    pool, me = lax.optimization_barrier((fill_pool(arrived), me))
    return assemble(me, pieces), pool


def solution(mesh):
    in_specs = (
        P("replica", "tensor"),
        P("replica", "tensor"),
        P("replica", "tensor"),
        P("replica", None),
        P("replica", None),
        P("replica", None),
        P(),
        P(),
    )
    out_specs = (P(("replica", "tensor"), None), P("replica", None, "tensor"))
    return jax.shard_map(shards, mesh=mesh, in_specs=in_specs, out_specs=out_specs, check_vma=False)
```
